256 devices in a mesh: tile: 64 (over z_lo, y, x, core), chol: 4 (over z_hi).
Axes of the slice: x: 4, y: 4, z: 8 (z_hi: 4, z_lo: 2; z = z_hi * 2 + z_lo), core: 2. Of those that a mesh axis runs over, the one named last changes fastest.
Arguments:
- chol_a: bfloat16 [4096, 64, 1024], P('chol', None, 'tile'), may hold values from -6 to 6
- chol_b: bfloat16 [4096, 4, 1024], P('chol', None, 'tile'), may hold values from -0.09375 to 0.09375
- amplitudes: bfloat16 [256, 1024, 1024], P(None, 'tile'), may hold values from -0.015625 to 0.015625
- virt_irrep: int32 [64], replicated, may hold values from 0 to 7
- pair_irrep: int32 [256], replicated, may hold values from 0 to 7
Outputs:
- ladder: float32 [256, 256], P('tile')
The draws below stay inside these ranges and needn't reach their ends.
All inputs are finite; a program needn't handle non-finite values.
Results may differ from the reference program's by a relative error of at most 0.017.
Values may be sent and summed in bfloat16 or wider, within the bound.
A program may use at most 128 MiB of HBM per device.

```python
import jax
import jax.numpy as jnp
from jax import lax

NCHOL = 4096
VW = 1024
VBLK = 16
AROWS = 64
BROWS = 4
IJ = 256


def plant(entries, own_key, least, top_value):
    longest = entries.shape.index(max(entries.shape))
    spots = []
    for shift in (0, 1):
        where = [jax.random.randint(jax.random.fold_in(own_key, axis), (), 0, length) for axis, length in enumerate(entries.shape)]
        where[longest] = (where[longest] + shift) % entries.shape[longest]
        spots.append(tuple(where))
    return entries.at[spots[0]].set(least).at[spots[1]].set(top_value)


def level_of(key, dims, split, smallest, high):
    loudness, own = 1.0, jax.random.fold_in(key, 6)
    for dim, shards_of in split:
        draws = jnp.exp(jax.random.uniform(jax.random.fold_in(own, dim), (shards_of,), jnp.float32, smallest / len(split), high / len(split)))
        loudness = loudness * jnp.repeat(draws, dims[dim] // shards_of).reshape([-1 if axis == dim else 1 for axis in range(len(dims))])
    return loudness


def centred(rng, extent, width, bound, split=(), held_as=jnp.bfloat16):
    array = width * jax.random.normal(rng, extent, jnp.float32)
    if split:
        array = array * level_of(rng, extent, split, -0.22, 0.18)
    return jnp.clip(array, -bound, bound).astype(held_as)


def setup_inputs(seed: int = 0) -> dict:
    keys = jax.random.split(jax.random.key(seed), 6)
    return {
        "chol_a": centred(keys[0], (NCHOL, AROWS, VW), 1.0, 6.0, ((0, 4), (2, 64))),
        "chol_b": centred(keys[1], (NCHOL, BROWS, VW), NCHOL ** -0.5, 0.09375, ((0, 4), (2, 64))),
        "amplitudes": centred(keys[2], (IJ, VW, VW), (VW * VW // 8) ** -0.5, 0.015625, ((1, 64),)),
        "virt_irrep": plant(jax.random.randint(keys[3], (VW // VBLK,), 0, 8), jax.random.fold_in(keys[3], 1), 0, 7).astype(jnp.int32),
        "pair_irrep": plant(jax.random.randint(keys[4], (IJ,), 0, 8), jax.random.fold_in(keys[4], 1), 0, 7).astype(jnp.int32),
    }


def reference(chol_a, chol_b, amplitudes, virt_irrep, pair_irrep):
    vec_count, a_rows, virt_count = chol_a.shape
    b_rows = chol_b.shape[1]
    pair_count = amplitudes.shape[0]
    span_cols = 64
    left_rows = chol_a.reshape(vec_count, a_rows * virt_count)
    labels = virt_irrep[jnp.arange(virt_count, dtype=jnp.int32) // VBLK]

    def advance(running, position):
        offset = (position * span_cols).astype(jnp.int32)
        factor = lax.dynamic_slice_in_dim(chol_b, offset, span_cols, 2).reshape(vec_count, b_rows * span_cols)
        integral = lax.dot_general(left_rows, factor, (((0,), (0,)), ((), ())), preferred_element_type=jnp.float32)
        integral = integral.astype(jnp.bfloat16).reshape(a_rows, virt_count, b_rows, span_cols)
        amp_block = lax.dynamic_slice_in_dim(amplitudes, offset, span_cols, 2)
        col_labels = lax.dynamic_slice_in_dim(labels, offset, span_cols, 0)
        allowed = jnp.bitwise_xor(labels[:, None], col_labels[None, :])[None, :, :] == pair_irrep[:, None, None]
        masked = jnp.where(allowed, amp_block, jnp.zeros_like(amp_block))
        update = jnp.einsum("icd,acbd->iab", masked.astype(jnp.float32), integral.astype(jnp.float32), precision=lax.Precision.HIGHEST)
        return running + update.reshape(pair_count, a_rows * b_rows), None

    initial = jnp.zeros((pair_count, a_rows * b_rows), jnp.float32)
    running, _ = lax.scan(advance, initial, jnp.arange(virt_count // span_cols, dtype=jnp.int32))
    return running
```

```python
import jax
import jax.numpy as jnp
from jax import lax
from jax.experimental import pallas as pl
from jax.experimental.pallas import tpu as pltpu
from jax.sharding import PartitionSpec as P

F32, BF16 = jnp.float32, jnp.bfloat16
MESH = pl.DeviceIdType.MESH
NT = (((1,), (1,)), ((), ()))
CHUNKS = 8
PART = {"X": (0, 512), "Y": (512, 512)}
MOVES = [
    ('y+', 'X', 0, 0, 0, None),
    ('y-', 'X', 0, 0, 0, None),
    ('y+', 'X', 0, 3, 0, 0),
    ('y-', 'X', 0, 1, 0, 1),
    ('z', 'X', 0, 0, 0, None),
    ('z', 'X', 0, 1, 0, None),
    ('z', 'X', 0, 3, 0, None),
    ('z', 'X', 0, 2, 0, None),
    ('z', 'X', 0, 0, 1, None),
    ('z', 'X', 0, 0, 3, None),
    ('x+', 'X', 0, 0, 0, None),
    ('x-', 'X', 0, 0, 0, None),
    ('x+', 'X', 0, 1, 0, None),
    ('x-', 'X', 0, 1, 0, None),
    ('x+', 'X', 0, 3, 0, None),
    ('x-', 'X', 0, 3, 0, None),
    ('x+', 'X', 0, 2, 0, None),
    ('x-', 'X', 0, 2, 0, None),
    ('x+', 'X', 1, 1, 0, None),
    ('x-', 'X', 1, 1, 0, None),
    ('x+', 'X', 1, 3, 0, None),
    ('x-', 'X', 1, 3, 0, None),
    ('x+', 'X', 1, 2, 0, None),
    ('x-', 'X', 1, 2, 0, None),
    ('x+', 'X', 0, 0, 3, None),
    ('x-', 'X', 1, 0, 1, None),
    ('x+', 'X', 0, 1, 3, None),
    ('x-', 'X', 1, 1, 1, None),
    ('x+', 'X', 0, 3, 3, None),
    ('x-', 'X', 1, 3, 1, None),
    ('x+', 'X', 0, 2, 3, None),
    ('x-', 'X', 1, 2, 1, None),
    ('x+', 'Y', 0, 0, 0, None),
    ('x-', 'Y', 0, 0, 0, None),
    ('x+', 'Y', 0, 0, 3, 0),
    ('x-', 'Y', 0, 0, 1, 1),
    ('z', 'Y', 0, 0, 0, None),
    ('z', 'Y', 0, 0, 1, None),
    ('z', 'Y', 0, 0, 3, None),
    ('z', 'Y', 0, 0, 2, None),
    ('z', 'Y', 0, 1, 0, None),
    ('z', 'Y', 0, 3, 0, None),
    ('y+', 'Y', 0, 0, 0, None),
    ('y-', 'Y', 0, 0, 0, None),
    ('y+', 'Y', 0, 0, 1, None),
    ('y-', 'Y', 0, 0, 1, None),
    ('y+', 'Y', 0, 0, 3, None),
    ('y-', 'Y', 0, 0, 3, None),
    ('y+', 'Y', 0, 0, 2, None),
    ('y-', 'Y', 0, 0, 2, None),
    ('y+', 'Y', 1, 0, 1, None),
    ('y-', 'Y', 1, 0, 1, None),
    ('y+', 'Y', 1, 0, 3, None),
    ('y-', 'Y', 1, 0, 3, None),
    ('y+', 'Y', 1, 0, 2, None),
    ('y-', 'Y', 1, 0, 2, None),
    ('y+', 'Y', 0, 3, 0, None),
    ('y-', 'Y', 1, 1, 0, None),
    ('y+', 'Y', 0, 3, 1, None),
    ('y-', 'Y', 1, 1, 1, None),
    ('y+', 'Y', 0, 3, 3, None),
    ('y-', 'Y', 1, 1, 3, None),
    ('y+', 'Y', 0, 3, 2, None),
    ('y-', 'Y', 1, 1, 2, None),
    ('c', 'X', 0, 0, None, None),
    ('c', 'Y', 0, 0, None, None),
    ('c', 'X', 1, 0, None, None),
    ('c', 'Y', 1, 0, None, None),
    ('c', 'X', 0, 1, None, None),
    ('c', 'Y', 0, 1, None, None),
    ('c', 'X', 1, 1, None, None),
    ('c', 'Y', 1, 1, None, None),
    ('c', 'X', 0, 3, None, None),
    ('c', 'Y', 0, 3, None, None),
    ('c', 'X', 1, 3, None, None),
    ('c', 'Y', 1, 3, None, None),
    ('c', 'X', 0, 2, None, None),
    ('c', 'Y', 0, 2, None, None),
    ('c', 'X', 1, 2, None, None),
    ('c', 'Y', 1, 2, None, None),
]
BEFORE_LEFT = [
    [],
    [],
    [],
    [],
]
BEFORE_AMPS = [
    [],
    [],
    [],
    [],
    [],
    [],
    [],
    [('barrier', 0), ('send', 1), ('send', 11), ('send', 36), ('send', 42), ('send', 32), ('send', 0), ('send', 10), ('send', 43), ('send', 33), ('send', 4)],
    [],
    [],
    [],
    [],
    [],
    [],
    [],
    [],
]
BEFORE_HALF = [
    [
        [('wait', 1), ('send', 5), ('send', 12), ('send', 3), ('send', 13), ('wait', 11), ('send', 8), ('wait', 36), ('wait', 42), ('send', 56), ('wait', 32), ('send', 47), ('send', 46), ('send', 34), ('send', 38), ('wait', 43), ('wait', 33), ('send', 44), ('send', 35), ('send', 45), ('wait', 4), ('wait', 0), ('send', 14), ('send', 15), ('wait', 10), ('send', 24), ('send', 37), ('send', 2), ('wait', 3), ('wait', 5), ('send', 19), ('send', 18), ('wait', 12), ('wait', 13), ('wait', 56), ('send', 9), ('wait', 34), ('wait', 47), ('wait', 35), ('send', 65), ('send', 49), ('send', 48), ('send', 26), ('wait', 8), ('send', 25), ('wait', 46), ('send', 60), ('send', 39), ('wait', 65), ('wait', 14), ('wait', 45), ('wait', 15), ('send', 28), ('wait', 38), ('send', 52), ('send', 53), ('wait', 44), ('send', 6), ('wait', 24), ('send', 64), ('wait', 19), ('send', 27), ('wait', 2), ('send', 17), ('wait', 49), ('send', 69), ('send', 16), ('send', 58), ('wait', 37), ('send', 51), ('send', 7), ('wait', 64)],
        [('wait', 26), ('send', 68), ('wait', 60), ('wait', 27), ('send', 70), ('wait', 73), ('send', 62), ('wait', 39), ('send', 67), ('send', 55), ('wait', 51), ('send', 59), ('wait', 66), ('send', 41), ('wait', 28), ('send', 72), ('wait', 68), ('wait', 52), ('wait', 17), ('send', 54), ('wait', 70), ('wait', 6), ('send', 21), ('send', 20), ('wait', 67)],
        [],
        [('wait', 62), ('send', 77), ('wait', 71)],
        [('wait', 63), ('wait', 22), ('wait', 76)],
        [('wait', 74), ('wait', 31), ('send', 78)],
        [],
        [],
    ],
    [
        [('wait', 18), ('wait', 25), ('wait', 69), ('wait', 48), ('send', 73), ('send', 50)],
        [('wait', 72), ('wait', 16), ('send', 30), ('wait', 61), ('wait', 58)],
        [('wait', 55), ('send', 63), ('wait', 50), ('wait', 40), ('send', 57), ('send', 71)],
        [('wait', 41), ('wait', 30), ('send', 76), ('wait', 23), ('send', 31)],
        [('wait', 29), ('send', 74), ('wait', 75)],
        [('wait', 79)],
        [],
        [],
    ],
]
BEFORE_FOLD = [
    [('send', 40), ('wait', 9), ('send', 66), ('wait', 53), ('send', 61)],
    [('wait', 7), ('send', 22), ('send', 23)],
    [('wait', 21), ('send', 29), ('wait', 20), ('wait', 59)],
    [('wait', 54), ('send', 75), ('wait', 77)],
    [('wait', 57), ('send', 79)],
    [('wait', 78)],
    [],
    [],
]


class Place:
    def __init__(self):
        self.tile, self.chol = lax.axis_index("tile"), lax.axis_index("chol")
        self.core = lax.rem(self.tile, 2)
        self.x = lax.rem(lax.div(self.tile, 2), 4)
        self.y = lax.rem(lax.div(self.tile, 8), 4)
        self.z = lax.div(self.tile, 32)
        self.xy = self.y * 4 + self.x
        self.slab = self.chol * 2 + self.z

    def device(self, z, y, x, core, chol=None):
        return (((z * 4 + y) * 4 + x) * 2 + core, self.chol if chol is None else chol)

    def neighbour(self, link):
        z, y, x, core = self.z, self.y, self.x, self.core
        if link == "z":
            return self.device(1 - z, y, x, core)
        if link == "c":
            return self.device(z, y, x, 1 - core)
        step = 1 if link[1] == "+" else 3
        if link[0] == "x":
            return self.device(z, y, lax.rem(x + step, 4), core)
        return self.device(z, lax.rem(y + step, 4), x, core)

    def in_plane(self, other):
        return self.device(self.z, lax.div(other, 4), lax.rem(other, 4), self.core)

    def on_column(self, other):
        return self.device(lax.rem(other, 2), self.y, self.x, self.core, lax.div(other, 2))


def region(held, at, part, dz, dy, dx, half, core):
    z, y = lax.rem(at.z + dz, 2), lax.rem(at.y + dy, 4)
    x = slice(None) if dx is None else lax.rem(at.x + dx, 4)
    cols = PART[part]
    rows = slice(None) if half is None else pl.ds(2 * half, 2)
    return held.at[rows, z, y, x, core, :, pl.ds(cols[0], cols[1])]


def received(link, dz, dy, dx):
    if link == "z":
        return 1 - dz, dy, dx
    if link == "c":
        return dz, dy, dx
    step = 3 if link[1] == "+" else 1
    if link[0] == "x":
        return dz, dy, (dx + step) % 4
    return dz, (dy + step) % 4, dx


def transfer(at, held, send_sems, recv_sems, number, incoming):
    link, part, dz, dy, dx, half = MOVES[number]
    core = at.core
    if incoming:
        dz, dy, dx = received(link, dz, dy, dx)
        core = 1 - core if link == "c" else core
    block = region(held, at, part, dz, dy, dx, half, core)
    return pltpu.make_async_remote_copy(
        src_ref=block,
        dst_ref=block,
        send_sem=send_sems.at[number],
        recv_sem=recv_sems.at[number],
        device_id=at.neighbour(link),
        device_id_type=MESH,
    )


def chunk_of(at, step):
    turn = lax.div(step, 2)
    dy = turn + lax.div(turn, 2) - 2 * lax.div(turn, 3)
    return lax.rem(at.z + lax.rem(step, 2), 2), lax.rem(at.y + dy, 4)


def kernel(
    chol_a, chol_b, amps, virt, pair, out,
    held, left, amps_in, amps_c, mask, integral, acc,
    halves, plane_out, plane_in, column_out, column_in, left_in,
    send_sems, recv_sems, load_sems, half_sems, plane_sems, column_sems,
):
    at = Place()
    loads = [
        pltpu.make_async_copy(chol_b, held.at[:, at.z, at.y, at.x, at.core], load_sems.at[0]),
        pltpu.make_async_copy(chol_a, left_in, load_sems.at[1]),
    ]
    for piece in range(8):
        rows = pl.ds((piece // 2 + 4 * (piece % 2)) * 32, 32)
        loads.append(pltpu.make_async_copy(amps.at[rows], amps_in.at[rows], load_sems.at[2 + piece]))
    for load in loads:
        load.start()
    barrier = pltpu.get_barrier_semaphore()
    peers = [at.neighbour("c")]
    peers += [at.in_plane(lax.rem(at.xy + step, 16)) for step in range(1, 16)]
    peers += [at.on_column(lax.rem(at.slab + step, 8)) for step in range(1, 8)]
    for peer in peers:
        pl.semaphore_signal(barrier, inc=1, device_id=peer, device_id_type=MESH)

    def move(kind, number):
        copy = transfer(at, held, send_sems, recv_sems, number, kind == "wait")
        if kind == "send":
            copy.start()
        else:
            copy.wait_recv()

    def moves(table, step):
        for turn, entries in enumerate(table):
            if entries:

                @pl.when(step == turn)
                def _():
                    for kind, number in entries:
                        if kind == "barrier":
                            loads[0].wait()
                            pl.semaphore_wait(barrier, len(peers))
                        else:
                            move(kind, number)

    def iota(shape, dim):
        return lax.broadcasted_iota(jnp.int32, shape, dim)

    virt_row = jnp.broadcast_to(virt[...], (8, 64)).astype(F32).astype(BF16)
    spread = (lax.div(iota((64, 1024), 1), 16) == iota((64, 1024), 0)).astype(F32).astype(BF16)
    own = (iota((64, 1024), 0) == at.tile).astype(F32).astype(BF16)
    label = jnp.dot(virt_row, spread, preferred_element_type=F32).astype(jnp.int32)
    mine = jnp.dot(virt_row, own, preferred_element_type=F32).astype(jnp.int32)
    wanted = jnp.bitwise_xor(label, mine)[:1]
    row = iota((256, 256), 0)
    source = (
        lax.rem(lax.div(row, 4), 2) * 128 + lax.div(row, 16) * 8
        + lax.rem(lax.div(row, 8), 2) * 4 + lax.rem(row, 4)
    )
    order = (iota((256, 256), 1) == source).astype(F32).astype(BF16)
    pair_row = jnp.broadcast_to(pair[...], (128, 256)).astype(F32).astype(BF16)
    pair_col = lax.dot_general(order, pair_row, NT, preferred_element_type=F32).astype(jnp.int32)
    for chunk in range(CHUNKS):
        cols = slice(chunk * 128, (chunk + 1) * 128)
        mask[chunk] = (pair_col == wanted[:, cols]).astype(F32).astype(BF16)
    acc[...] = jnp.zeros_like(acc)

    loads[1].wait()

    @pl.loop(0, 4)
    def _(group):
        moves(BEFORE_LEFT, group)
        rows = pl.ds(pl.multiple_of(group * 16, 16), 16)
        for cols in range(0, 1024, 128):
            block = left_in[rows, :, cols : cols + 128]
            left[:, rows, cols : cols + 128] = jnp.swapaxes(block, 0, 1)

    @pl.loop(0, 16)
    def _(group):
        for piece in range(4):

            @pl.when(group == 4 * piece)
            def _():
                loads[2 + 2 * piece].wait()
                loads[3 + 2 * piece].wait()

        moves(BEFORE_AMPS, group)
        rows = pl.ds(pl.multiple_of(group * 16, 16), 16)
        for chunk in range(CHUNKS):
            cols = slice(chunk * 128, (chunk + 1) * 128)
            block = jnp.concatenate(
                [
                    amps_in[pl.ds(128 * z + group * 8 + 4 * core, 4), :, cols]
                    for core in range(2)
                    for z in range(2)
                ],
                0,
            )
            amps_c[chunk, :, rows, :] = jnp.swapaxes(block, 0, 1) * mask[chunk, rows, :][None]

    @pl.loop(0, CHUNKS)
    def _(step):
        z, y = chunk_of(at, step)
        for half in range(2):
            moves(BEFORE_HALF[half], step)
            vectors = held[2 * half : 2 * half + 2, z, y].reshape(256, 1024)
            block = lax.dot_general(
                left[...].reshape(1024, 1024), vectors, NT, preferred_element_type=F32
            ).astype(BF16)
            for c in range(16):
                for b in range(2):
                    integral[(2 * half + b) * 64 : (2 * half + b + 1) * 64, c * 128 : (c + 1) * 128] = (
                        block[c * 64 : (c + 1) * 64, b * 128 : (b + 1) * 128]
                    )
        moves(BEFORE_FOLD, step)
        masked = jnp.concatenate([amps_c[z * 4 + y, c] for c in range(16)], 1)
        acc[...] += lax.dot_general(
            masked, integral[...], NT, preferred_element_type=F32
        ).reshape(16, 2, 8, 256)

    swap = pltpu.make_async_remote_copy(
        src_ref=acc.at[:, 1 - at.core],
        dst_ref=halves,
        send_sem=half_sems.at[0],
        recv_sem=half_sems.at[1],
        device_id=at.neighbour("c"),
        device_id_type=MESH,
    )
    swap.start()
    turn = (
        (lax.rem(iota((256, 256), 0), 64) == lax.div(iota((256, 256), 1), 4))
        & (lax.div(iota((256, 256), 0), 64) == lax.rem(iota((256, 256), 1), 4))
    ).astype(F32).astype(BF16)
    swap.wait_recv()
    pairs = (acc[:, at.core] + halves[...]).reshape(128, 256).astype(BF16)
    pairs = jnp.dot(pairs, turn, preferred_element_type=F32).reshape(16, 8, 256)
    plane_out[...] = jnp.concatenate([pairs[:, :, :128], pairs[:, :, 128:]], 1).astype(BF16)
    copies = []
    for step in range(1, 16):
        other = lax.rem(at.xy + step, 16)
        copies.append(
            pltpu.make_async_remote_copy(
                src_ref=plane_out.at[other],
                dst_ref=plane_in.at[at.xy],
                send_sem=plane_sems.at[0, other],
                recv_sem=plane_sems.at[1, at.xy],
                device_id=at.in_plane(other),
                device_id_type=MESH,
            )
        )
        copies[-1].start()
    total = plane_out[at.xy].astype(F32)
    for step in range(1, 16):
        other = lax.rem(at.xy + step, 16)
        pltpu.make_async_remote_copy(
            src_ref=plane_out.at[other],
            dst_ref=plane_in.at[other],
            send_sem=plane_sems.at[0, other],
            recv_sem=plane_sems.at[1, other],
            device_id=at.in_plane(other),
            device_id_type=MESH,
        ).wait_recv()
        total += plane_in[other].astype(F32)
    column_out[...] = total.astype(BF16)
    for step in range(1, 8):
        other = lax.rem(at.slab + step, 8)
        copies.append(
            pltpu.make_async_remote_copy(
                src_ref=column_out,
                dst_ref=column_in.at[at.slab],
                send_sem=column_sems.at[0, other],
                recv_sem=column_sems.at[1, at.slab],
                device_id=at.on_column(other),
                device_id_type=MESH,
            )
        )
        copies[-1].start()
    total = column_out[...].astype(F32)
    for step in range(1, 8):
        other = lax.rem(at.slab + step, 8)
        pltpu.make_async_remote_copy(
            src_ref=column_out,
            dst_ref=column_in.at[other],
            send_sem=column_sems.at[0, other],
            recv_sem=column_sems.at[1, other],
            device_id=at.on_column(other),
            device_id_type=MESH,
        ).wait_recv()
        total += column_in[other].astype(F32)
    total = jnp.where(at.z == 0, total.reshape(2, 2, 4, 128)[:, 0], total.reshape(2, 2, 4, 128)[:, 1])
    out[:, :128] = total[0]
    out[:, 128:] = total[1]
    for number in range(len(MOVES)):
        transfer(at, held, send_sems, recv_sems, number, False).wait_send()
    swap.wait_send()
    for copy in copies:
        copy.wait_send()


def body(chol_a, chol_b, amplitudes, virt_irrep, pair_irrep):
    vec, a_rows, c_rows = chol_a.shape
    b_rows = chol_b.shape[1]
    pairs, _, virt = amplitudes.shape
    anywhere = pl.BlockSpec(memory_space=pl.ANY)
    inside = pl.BlockSpec(memory_space=pltpu.VMEM)
    dma = pltpu.SemaphoreType.DMA
    return pl.pallas_call(
        kernel,
        out_shape=jax.ShapeDtypeStruct((4, 256), F32),
        in_specs=[anywhere, anywhere, anywhere, inside, inside],
        out_specs=inside,
        scratch_shapes=[
            pltpu.VMEM((b_rows, 2, 4, 4, 2, 16, vec), BF16),
            pltpu.VMEM((c_rows, a_rows, vec), BF16),
            pltpu.VMEM((pairs, c_rows, virt), BF16),
            pltpu.VMEM((CHUNKS, c_rows, pairs, 128), BF16),
            pltpu.VMEM((CHUNKS, pairs, 128), BF16),
            pltpu.VMEM((256, 2048), BF16),
            pltpu.VMEM((16, 2, 8, 256), F32),
            pltpu.VMEM((16, 8, 256), F32),
            pltpu.VMEM((16, 16, 128), BF16),
            pltpu.VMEM((16, 16, 128), BF16),
            pltpu.VMEM((16, 128), BF16),
            pltpu.VMEM((8, 16, 128), BF16),
            pltpu.VMEM((a_rows, c_rows, vec), BF16),
            dma((len(MOVES),)),
            dma((len(MOVES),)),
            dma((10,)),
            dma((2,)),
            dma((2, 16)),
            dma((2, 8)),
        ],
        compiler_params=pltpu.CompilerParams(
            collective_id=0, has_side_effects=True, vmem_limit_bytes=56 * 2**20
        ),
        name="ladder",
    )(
        jnp.transpose(chol_a, (1, 2, 0)),
        jnp.transpose(chol_b, (1, 2, 0)),
        amplitudes,
        virt_irrep.reshape(1, -1),
        pair_irrep.reshape(1, -1),
    )


def solution(mesh):
    placed = (P("chol", None, "tile"), P("chol", None, "tile"), P(None, "tile", None), P(), P())
    return jax.shard_map(
        body, mesh=mesh, in_specs=placed, out_specs=P("tile", None), check_vma=False
    )
```

```python
import jax
import jax.numpy as jnp
from jax import lax
from jax.experimental import pallas as pl
from jax.experimental.pallas import tpu as pltpu
from jax.sharding import PartitionSpec as P

F32, BF16 = jnp.float32, jnp.bfloat16
MESH = pl.DeviceIdType.MESH
NT = (((1,), (1,)), ((), ()))
CHUNKS = 8
PART = {"X": (0, 512), "Y": (512, 512)}
MOVES = [
    ('y+', 'X', 0, 0, 0, None),
    ('y-', 'X', 0, 0, 0, None),
    ('y+', 'X', 0, 3, 0, 0),
    ('y-', 'X', 0, 1, 0, 1),
    ('z', 'X', 0, 0, 0, None),
    ('z', 'X', 0, 1, 0, None),
    ('z', 'X', 0, 3, 0, None),
    ('z', 'X', 0, 2, 0, None),
    ('x+', 'X', 0, 0, 0, None),
    ('x-', 'X', 0, 0, 0, None),
    ('x+', 'X', 0, 1, 0, None),
    ('x-', 'X', 0, 1, 0, None),
    ('x+', 'X', 0, 3, 0, None),
    ('x-', 'X', 0, 3, 0, None),
    ('x+', 'X', 0, 2, 0, None),
    ('x-', 'X', 0, 2, 0, None),
    ('x+', 'X', 1, 0, 0, None),
    ('x-', 'X', 1, 0, 0, None),
    ('x+', 'X', 1, 1, 0, None),
    ('x-', 'X', 1, 1, 0, None),
    ('x+', 'X', 1, 3, 0, None),
    ('x-', 'X', 1, 3, 0, None),
    ('x+', 'X', 1, 2, 0, None),
    ('x-', 'X', 1, 2, 0, None),
    ('x+', 'X', 0, 0, 3, None),
    ('x-', 'X', 1, 0, 1, None),
    ('x+', 'X', 0, 1, 3, None),
    ('x-', 'X', 1, 1, 1, None),
    ('x+', 'X', 0, 3, 3, None),
    ('x-', 'X', 1, 3, 1, None),
    ('x+', 'X', 0, 2, 3, None),
    ('x-', 'X', 1, 2, 1, None),
    ('x+', 'Y', 0, 0, 0, None),
    ('x-', 'Y', 0, 0, 0, None),
    ('x+', 'Y', 0, 0, 3, 0),
    ('x-', 'Y', 0, 0, 1, 1),
    ('z', 'Y', 0, 0, 0, None),
    ('z', 'Y', 0, 0, 1, None),
    ('z', 'Y', 0, 0, 3, None),
    ('z', 'Y', 0, 0, 2, None),
    ('y+', 'Y', 0, 0, 0, None),
    ('y-', 'Y', 0, 0, 0, None),
    ('y+', 'Y', 0, 0, 1, None),
    ('y-', 'Y', 0, 0, 1, None),
    ('y+', 'Y', 0, 0, 3, None),
    ('y-', 'Y', 0, 0, 3, None),
    ('y+', 'Y', 0, 0, 2, None),
    ('y-', 'Y', 0, 0, 2, None),
    ('y+', 'Y', 1, 0, 0, None),
    ('y-', 'Y', 1, 0, 0, None),
    ('y+', 'Y', 1, 0, 1, None),
    ('y-', 'Y', 1, 0, 1, None),
    ('y+', 'Y', 1, 0, 3, None),
    ('y-', 'Y', 1, 0, 3, None),
    ('y+', 'Y', 1, 0, 2, None),
    ('y-', 'Y', 1, 0, 2, None),
    ('y+', 'Y', 0, 3, 0, None),
    ('y-', 'Y', 1, 1, 0, None),
    ('y+', 'Y', 0, 3, 1, None),
    ('y-', 'Y', 1, 1, 1, None),
    ('y+', 'Y', 0, 3, 3, None),
    ('y-', 'Y', 1, 1, 3, None),
    ('y+', 'Y', 0, 3, 2, None),
    ('y-', 'Y', 1, 1, 2, None),
    ('c', 'X', 0, 0, None, None),
    ('c', 'Y', 0, 0, None, None),
    ('c', 'X', 1, 0, None, None),
    ('c', 'Y', 1, 0, None, None),
    ('c', 'X', 0, 1, None, None),
    ('c', 'Y', 0, 1, None, None),
    ('c', 'X', 1, 1, None, None),
    ('c', 'Y', 1, 1, None, None),
    ('c', 'X', 0, 3, None, None),
    ('c', 'Y', 0, 3, None, None),
    ('c', 'X', 1, 3, None, None),
    ('c', 'Y', 1, 3, None, None),
    ('c', 'X', 0, 2, None, None),
    ('c', 'Y', 0, 2, None, None),
    ('c', 'X', 1, 2, None, None),
    ('c', 'Y', 1, 2, None, None),
]
FIRST = [('send', 4), ('send', 33), ('send', 1), ('send', 32), ('send', 0)]
BEFORE_LEFT = [
    [('send', 36), ('send', 8), ('send', 9), ('send', 40), ('send', 41)],
    [],
    [],
    [],
]
BEFORE_AMPS = [
    [],
    [],
    [],
    [],
    [],
    [],
    [('wait', 4), ('send', 16), ('send', 17), ('wait', 33), ('send', 43), ('send', 42), ('send', 37), ('wait', 1), ('wait', 32), ('send', 34), ('send', 35), ('wait', 0), ('send', 45), ('send', 2), ('send', 38)],
    [],
    [],
    [('send', 13), ('send', 10), ('send', 44)],
    [],
    [('wait', 36), ('wait', 9), ('wait', 41), ('wait', 8), ('wait', 40)],
    [('send', 49), ('send', 5)],
    [],
    [('send', 24), ('send', 48), ('send', 11)],
    [],
]
BEFORE_CHUNK = [
    [('wait', 16), ('wait', 17), ('wait', 43), ('send', 3), ('wait', 42), ('send', 6), ('wait', 37), ('wait', 34), ('send', 12), ('send', 25), ('wait', 35), ('send', 47), ('send', 46), ('send', 65), ('wait', 2), ('wait', 45), ('wait', 38), ('send', 39), ('wait', 10), ('send', 26), ('wait', 13), ('send', 51), ('send', 50), ('wait', 44), ('wait', 49), ('wait', 5), ('send', 19), ('wait', 24), ('send', 18), ('send', 64), ('wait', 11), ('send', 57), ('send', 58), ('wait', 3), ('send', 7), ('send', 15), ('wait', 48), ('wait', 6), ('wait', 12), ('send', 14), ('send', 21), ('wait', 25), ('send', 66), ('send', 52), ('send', 53), ('wait', 64), ('wait', 65)],
    [('send', 20), ('send', 60), ('wait', 47), ('send', 69), ('wait', 46), ('send', 73), ('wait', 39), ('send', 67), ('send', 55), ('wait', 26), ('send', 68), ('wait', 19), ('send', 27), ('wait', 51), ('wait', 50), ('wait', 7), ('wait', 18), ('send', 28), ('send', 23), ('wait', 15), ('send', 59), ('send', 54), ('wait', 57), ('wait', 58), ('wait', 66), ('wait', 67)],
    [('send', 62), ('send', 22), ('wait', 14), ('wait', 21), ('send', 29), ('wait', 53), ('send', 61), ('wait', 52), ('send', 56), ('send', 30), ('wait', 20), ('wait', 27), ('send', 70), ('wait', 55), ('send', 71), ('send', 63), ('wait', 60), ('wait', 68), ('wait', 69)],
    [('wait', 28), ('send', 72), ('wait', 23), ('send', 31), ('wait', 59), ('wait', 54), ('send', 75), ('wait', 70), ('wait', 71)],
    [('wait', 62), ('wait', 22), ('wait', 29), ('send', 74), ('wait', 61), ('wait', 72), ('wait', 73)],
    [('wait', 56), ('send', 77), ('wait', 30), ('send', 76), ('wait', 63), ('send', 79), ('wait', 31), ('send', 78), ('wait', 74), ('wait', 75)],
    [('wait', 76), ('wait', 77)],
    [('wait', 78), ('wait', 79)],
]


class Place:
    def __init__(self):
        self.tile, self.chol = lax.axis_index("tile"), lax.axis_index("chol")
        self.core = lax.rem(self.tile, 2)
        self.x = lax.rem(lax.div(self.tile, 2), 4)
        self.y = lax.rem(lax.div(self.tile, 8), 4)
        self.z = lax.div(self.tile, 32)
        self.xy = self.y * 4 + self.x
        self.slab = self.chol * 2 + self.z

    def device(self, z, y, x, core, chol=None):
        return (((z * 4 + y) * 4 + x) * 2 + core, self.chol if chol is None else chol)

    def neighbour(self, link):
        z, y, x, core = self.z, self.y, self.x, self.core
        if link == "z":
            return self.device(1 - z, y, x, core)
        if link == "c":
            return self.device(z, y, x, 1 - core)
        step = 1 if link[1] == "+" else 3
        if link[0] == "x":
            return self.device(z, y, lax.rem(x + step, 4), core)
        return self.device(z, lax.rem(y + step, 4), x, core)

    def in_plane(self, other):
        return self.device(self.z, lax.div(other, 4), lax.rem(other, 4), self.core)

    def on_column(self, other):
        return self.device(lax.rem(other, 2), self.y, self.x, self.core, lax.div(other, 2))


def region(held, at, part, dz, dy, dx, half, core):
    z, y = lax.rem(at.z + dz, 2), lax.rem(at.y + dy, 4)
    x = slice(None) if dx is None else lax.rem(at.x + dx, 4)
    cols = PART[part]
    rows = slice(None) if half is None else pl.ds(2 * half, 2)
    return held.at[rows, z, y, x, core, :, pl.ds(cols[0], cols[1])]


def received(link, dz, dy, dx):
    if link == "z":
        return 1 - dz, dy, dx
    if link == "c":
        return dz, dy, dx
    step = 3 if link[1] == "+" else 1
    if link[0] == "x":
        return dz, dy, (dx + step) % 4
    return dz, (dy + step) % 4, dx


def transfer(at, held, send_sems, recv_sems, number, incoming):
    link, part, dz, dy, dx, half = MOVES[number]
    core = at.core
    if incoming:
        dz, dy, dx = received(link, dz, dy, dx)
        core = 1 - core if link == "c" else core
    block = region(held, at, part, dz, dy, dx, half, core)
    return pltpu.make_async_remote_copy(
        src_ref=block,
        dst_ref=block,
        send_sem=send_sems.at[number],
        recv_sem=recv_sems.at[number],
        device_id=at.neighbour(link),
        device_id_type=MESH,
    )


def chunk_of(at, step):
    turn = lax.div(step, 2)
    dy = turn + lax.div(turn, 2) - 2 * lax.div(turn, 3)
    return lax.rem(at.z + lax.rem(step, 2), 2), lax.rem(at.y + dy, 4)


def kernel(
    chol_a, chol_b, amps, virt, pair, out,
    held, left, amps_in, amps_c, mask, integral, acc,
    halves, plane_out, plane_in, column_out, column_in, left_in,
    heard_sems, send_sems, recv_sems, load_sems, half_sems, plane_sems, column_sems,
):
    at = Place()
    loads = [
        pltpu.make_async_copy(chol_b, held.at[:, at.z, at.y, at.x, at.core], load_sems.at[0]),
        pltpu.make_async_copy(chol_a, left_in, load_sems.at[1]),
    ]
    for piece in range(8):
        rows = pl.ds((piece // 2 + 4 * (piece % 2)) * 32, 32)
        loads.append(pltpu.make_async_copy(amps.at[rows], amps_in.at[rows], load_sems.at[2 + piece]))
    for load in loads:
        load.start()
    barrier = pltpu.get_barrier_semaphore()
    up, down = (at.on_column(lax.rem(at.slab + step, 8)) for step in (1, 7))
    peers = [at.neighbour(link) for link in ("c", "x+", "x-", "y+", "y-")] + [up, down]
    for peer in peers:
        pl.semaphore_signal(barrier, inc=1, device_id=peer, device_id_type=MESH)

    def hear(count):
        if count:
            pl.semaphore_wait(heard_sems.at[count - 1, 0], 1)
            pl.semaphore_wait(heard_sems.at[count - 1, 1], 1)
        if count < 3:
            pl.semaphore_signal(heard_sems.at[count, 0], inc=1, device_id=up, device_id_type=MESH)
            pl.semaphore_signal(heard_sems.at[count, 1], inc=1, device_id=down, device_id_type=MESH)

    def move(kind, number):
        copy = transfer(at, held, send_sems, recv_sems, number, kind == "wait")
        if kind == "send":
            copy.start()
        else:
            copy.wait_recv()

    def moves(table, step):
        for turn, entries in enumerate(table):
            if entries:
                if isinstance(step, int):
                    for kind, number in entries:
                        move(kind, number)
                    continue

                @pl.when(step == turn)
                def _():
                    for kind, number in entries:
                        move(kind, number)

    loads[0].wait()
    pl.semaphore_wait(barrier, len(peers))
    for kind, number in FIRST:
        move(kind, number)
    hear(0)

    def iota(shape, dim):
        return lax.broadcasted_iota(jnp.int32, shape, dim)

    virt_row = jnp.broadcast_to(virt[...], (8, 64)).astype(F32).astype(BF16)
    spread = (lax.div(iota((64, 1024), 1), 16) == iota((64, 1024), 0)).astype(F32).astype(BF16)
    own = (iota((64, 1024), 0) == at.tile).astype(F32).astype(BF16)
    label = jnp.dot(virt_row, spread, preferred_element_type=F32).astype(jnp.int32)
    mine = jnp.dot(virt_row, own, preferred_element_type=F32).astype(jnp.int32)
    wanted = jnp.bitwise_xor(label, mine)[:1]
    row = iota((256, 256), 0)
    source = (
        lax.rem(lax.div(row, 4), 2) * 128 + lax.div(row, 16) * 8
        + lax.rem(lax.div(row, 8), 2) * 4 + lax.rem(row, 4)
    )
    order = (iota((256, 256), 1) == source).astype(F32).astype(BF16)
    pair_row = jnp.broadcast_to(pair[...], (128, 256)).astype(F32).astype(BF16)
    pair_col = lax.dot_general(order, pair_row, NT, preferred_element_type=F32).astype(jnp.int32)
    for chunk in range(CHUNKS):
        cols = slice(chunk * 128, (chunk + 1) * 128)
        mask[chunk] = (pair_col == wanted[:, cols]).astype(F32).astype(BF16)
    acc[...] = jnp.zeros_like(acc)

    loads[1].wait()

    @pl.loop(0, 4)
    def _(group):
        moves(BEFORE_LEFT, group)
        rows = pl.ds(pl.multiple_of(group * 16, 16), 16)
        for cols in range(0, 1024, 128):
            block = left_in[rows, :, cols : cols + 128]
            left[:, rows, cols : cols + 128] = jnp.swapaxes(block, 0, 1)

    @pl.loop(0, 16)
    def _(group):
        for piece in range(4):

            @pl.when(group == 4 * piece)
            def _():
                loads[2 + 2 * piece].wait()
                loads[3 + 2 * piece].wait()

        for turn in (1, 2):

            @pl.when(group == 7 * turn)
            def _():
                hear(turn)

        moves(BEFORE_AMPS, group)
        rows = pl.ds(pl.multiple_of(group * 16, 16), 16)
        for chunk in range(CHUNKS):
            cols = slice(chunk * 128, (chunk + 1) * 128)
            block = jnp.concatenate(
                [
                    amps_in[pl.ds(128 * z + group * 8 + 4 * core, 4), :, cols]
                    for core in range(2)
                    for z in range(2)
                ],
                0,
            )
            amps_c[chunk, :, rows, :] = jnp.swapaxes(block, 0, 1) * mask[chunk, rows, :][None]

    def multiply(step):
        z, y = chunk_of(at, step)
        for half in range(2):
            vectors = held[2 * half : 2 * half + 2, z, y].reshape(256, 1024)
            block = lax.dot_general(
                left[...].reshape(1024, 1024), vectors, NT, preferred_element_type=F32
            ).astype(BF16)
            for c in range(16):
                for b in range(2):
                    integral[lax.rem(step, 2), pl.ds((2 * half + b) * 64, 64), pl.ds(c * 128, 128)] = (
                        block[c * 64 : (c + 1) * 64, b * 128 : (b + 1) * 128]
                    )

    def fold(step):
        z, y = chunk_of(at, step)
        masked = jnp.concatenate([amps_c[z * 4 + y, c] for c in range(16)], 1)
        acc[...] += lax.dot_general(
            masked, integral[lax.rem(step, 2)], NT, preferred_element_type=F32
        ).reshape(16, 2, 8, 256)

    moves(BEFORE_CHUNK[:1], 0)
    multiply(0)
    hear(3)

    @pl.loop(1, CHUNKS)
    def _(step):
        moves([[]] + BEFORE_CHUNK[1:], step)
        fold(step - 1)
        multiply(step)

    fold(CHUNKS - 1)

    swap = pltpu.make_async_remote_copy(
        src_ref=acc.at[:, 1 - at.core],
        dst_ref=halves,
        send_sem=half_sems.at[0],
        recv_sem=half_sems.at[1],
        device_id=at.neighbour("c"),
        device_id_type=MESH,
    )
    swap.start()
    turn = (
        (lax.rem(iota((256, 256), 0), 64) == lax.div(iota((256, 256), 1), 4))
        & (lax.div(iota((256, 256), 0), 64) == lax.rem(iota((256, 256), 1), 4))
    ).astype(F32).astype(BF16)
    swap.wait_recv()
    pairs = (acc[:, at.core] + halves[...]).reshape(128, 256).astype(BF16)
    pairs = jnp.dot(pairs, turn, preferred_element_type=F32).reshape(16, 8, 256)
    plane_out[...] = jnp.concatenate([pairs[:, :, :128], pairs[:, :, 128:]], 1).astype(BF16)
    copies = []
    for step in range(1, 16):
        other = lax.rem(at.xy + step, 16)
        copies.append(
            pltpu.make_async_remote_copy(
                src_ref=plane_out.at[other],
                dst_ref=plane_in.at[at.xy],
                send_sem=plane_sems.at[0, other],
                recv_sem=plane_sems.at[1, at.xy],
                device_id=at.in_plane(other),
                device_id_type=MESH,
            )
        )
        copies[-1].start()
    total = plane_out[at.xy].astype(F32)
    for step in range(1, 16):
        other = lax.rem(at.xy + step, 16)
        pltpu.make_async_remote_copy(
            src_ref=plane_out.at[other],
            dst_ref=plane_in.at[other],
            send_sem=plane_sems.at[0, other],
            recv_sem=plane_sems.at[1, other],
            device_id=at.in_plane(other),
            device_id_type=MESH,
        ).wait_recv()
        total += plane_in[other].astype(F32)
    column_out[...] = total.astype(BF16)
    for step in range(1, 8):
        other = lax.rem(at.slab + step, 8)
        copies.append(
            pltpu.make_async_remote_copy(
                src_ref=column_out,
                dst_ref=column_in.at[at.slab],
                send_sem=column_sems.at[0, other],
                recv_sem=column_sems.at[1, at.slab],
                device_id=at.on_column(other),
                device_id_type=MESH,
            )
        )
        copies[-1].start()
    total = column_out[...].astype(F32)
    for step in range(1, 8):
        other = lax.rem(at.slab + step, 8)
        pltpu.make_async_remote_copy(
            src_ref=column_out,
            dst_ref=column_in.at[other],
            send_sem=column_sems.at[0, other],
            recv_sem=column_sems.at[1, other],
            device_id=at.on_column(other),
            device_id_type=MESH,
        ).wait_recv()
        total += column_in[other].astype(F32)
    total = jnp.where(at.z == 0, total.reshape(2, 2, 4, 128)[:, 0], total.reshape(2, 2, 4, 128)[:, 1])
    out[:, :128] = total[0]
    out[:, 128:] = total[1]
    for number in range(len(MOVES)):
        transfer(at, held, send_sems, recv_sems, number, False).wait_send()
    swap.wait_send()
    for copy in copies:
        copy.wait_send()


def body(chol_a, chol_b, amplitudes, virt_irrep, pair_irrep):
    vec, a_rows, c_rows = chol_a.shape
    b_rows = chol_b.shape[1]
    pairs, _, virt = amplitudes.shape
    anywhere = pl.BlockSpec(memory_space=pl.ANY)
    inside = pl.BlockSpec(memory_space=pltpu.VMEM)
    dma = pltpu.SemaphoreType.DMA
    return pl.pallas_call(
        kernel,
        out_shape=jax.ShapeDtypeStruct((4, 256), F32),
        in_specs=[anywhere, anywhere, anywhere, inside, inside],
        out_specs=inside,
        scratch_shapes=[
            pltpu.VMEM((b_rows, 2, 4, 4, 2, 16, vec), BF16),
            pltpu.VMEM((c_rows, a_rows, vec), BF16),
            pltpu.VMEM((pairs, c_rows, virt), BF16),
            pltpu.VMEM((CHUNKS, c_rows, pairs, 128), BF16),
            pltpu.VMEM((CHUNKS, pairs, 128), BF16),
            pltpu.VMEM((2, 256, 2048), BF16),
            pltpu.VMEM((16, 2, 8, 256), F32),
            pltpu.VMEM((16, 8, 256), F32),
            pltpu.VMEM((16, 16, 128), BF16),
            pltpu.VMEM((16, 16, 128), BF16),
            pltpu.VMEM((16, 128), BF16),
            pltpu.VMEM((8, 16, 128), BF16),
            pltpu.VMEM((a_rows, c_rows, vec), BF16),
            pltpu.SemaphoreType.REGULAR((3, 2)),
            dma((len(MOVES),)),
            dma((len(MOVES),)),
            dma((10,)),
            dma((2,)),
            dma((2, 16)),
            dma((2, 8)),
        ],
        compiler_params=pltpu.CompilerParams(
            collective_id=0, has_side_effects=True, vmem_limit_bytes=56 * 2**20
        ),
        name="ladder",
    )(
        jnp.transpose(chol_a, (1, 2, 0)),
        jnp.transpose(chol_b, (1, 2, 0)),
        amplitudes,
        virt_irrep.reshape(1, -1),
        pair_irrep.reshape(1, -1),
    )


def solution(mesh):
    placed = (P("chol", None, "tile"), P("chol", None, "tile"), P(None, "tile", None), P(), P())
    return jax.shard_map(
        body, mesh=mesh, in_specs=placed, out_specs=P("tile", None), check_vma=False
    )
```

```python
import jax
import jax.numpy as jnp
from jax import lax
from jax.experimental import pallas as pl
from jax.experimental.pallas import tpu as pltpu
from jax.sharding import PartitionSpec as P

F32, BF16 = jnp.float32, jnp.bfloat16
MESH = pl.DeviceIdType.MESH
NT = (((1,), (1,)), ((), ()))
CHUNKS = 8
PART = {"X": (0, 512), "Y": (512, 512)}
MOVES = [
    ('y+', 'X', 0, 0, 0, None),
    ('y-', 'X', 0, 0, 0, None),
    ('y+', 'X', 0, 3, 0, 0),
    ('y-', 'X', 0, 1, 0, 1),
    ('z', 'X', 0, 0, 0, None),
    ('z', 'X', 0, 1, 0, None),
    ('z', 'X', 0, 3, 0, None),
    ('z', 'X', 0, 2, 0, None),
    ('x+', 'X', 0, 0, 0, None),
    ('x-', 'X', 0, 0, 0, None),
    ('x+', 'X', 0, 0, 3, 0),
    ('x-', 'X', 0, 0, 1, 1),
    ('x+', 'X', 0, 1, 0, None),
    ('x-', 'X', 0, 1, 0, None),
    ('x+', 'X', 0, 1, 3, None),
    ('x+', 'X', 0, 3, 0, None),
    ('x-', 'X', 0, 3, 0, None),
    ('x-', 'X', 0, 3, 1, None),
    ('x+', 'X', 0, 2, 0, None),
    ('x-', 'X', 0, 2, 0, None),
    ('x+', 'X', 0, 2, 3, None),
    ('x+', 'X', 1, 0, 0, None),
    ('x-', 'X', 1, 0, 0, None),
    ('x-', 'X', 1, 0, 1, None),
    ('x+', 'X', 1, 1, 0, None),
    ('x-', 'X', 1, 1, 0, None),
    ('x+', 'X', 1, 1, 3, None),
    ('x+', 'X', 1, 3, 0, None),
    ('x-', 'X', 1, 3, 0, None),
    ('x-', 'X', 1, 3, 1, None),
    ('x+', 'X', 1, 2, 0, None),
    ('x-', 'X', 1, 2, 0, None),
    ('x-', 'X', 1, 2, 1, None),
    ('x+', 'Y', 0, 0, 0, None),
    ('x-', 'Y', 0, 0, 0, None),
    ('x+', 'Y', 0, 0, 3, 0),
    ('x-', 'Y', 0, 0, 1, 1),
    ('z', 'Y', 0, 0, 0, None),
    ('z', 'Y', 0, 0, 1, None),
    ('z', 'Y', 0, 0, 3, None),
    ('z', 'Y', 0, 0, 2, None),
    ('y+', 'Y', 0, 0, 0, None),
    ('y-', 'Y', 0, 0, 0, None),
    ('y+', 'Y', 0, 3, 0, None),
    ('y+', 'Y', 0, 0, 1, None),
    ('y-', 'Y', 0, 0, 1, None),
    ('y-', 'Y', 0, 1, 1, None),
    ('y+', 'Y', 0, 0, 3, None),
    ('y-', 'Y', 0, 0, 3, None),
    ('y+', 'Y', 0, 3, 3, None),
    ('y+', 'Y', 0, 0, 2, None),
    ('y-', 'Y', 0, 0, 2, None),
    ('y-', 'Y', 0, 1, 2, None),
    ('y+', 'Y', 1, 0, 0, None),
    ('y-', 'Y', 1, 0, 0, None),
    ('y+', 'Y', 1, 3, 0, None),
    ('y+', 'Y', 1, 0, 1, None),
    ('y-', 'Y', 1, 0, 1, None),
    ('y-', 'Y', 1, 1, 1, None),
    ('y+', 'Y', 1, 0, 3, None),
    ('y-', 'Y', 1, 0, 3, None),
    ('y+', 'Y', 1, 3, 3, None),
    ('y+', 'Y', 1, 0, 2, None),
    ('y-', 'Y', 1, 0, 2, None),
    ('y-', 'Y', 1, 1, 2, None),
    ('c', 'X', 0, 0, None, None),
    ('c', 'Y', 0, 0, None, None),
    ('c', 'X', 0, 1, None, None),
    ('c', 'Y', 0, 1, None, None),
    ('c', 'X', 0, 3, None, None),
    ('c', 'Y', 0, 3, None, None),
    ('c', 'X', 1, 0, None, None),
    ('c', 'Y', 1, 0, None, None),
    ('c', 'X', 1, 1, None, None),
    ('c', 'Y', 1, 1, None, None),
    ('c', 'X', 1, 3, None, None),
    ('c', 'Y', 1, 3, None, None),
    ('c', 'X', 0, 2, None, None),
    ('c', 'Y', 0, 2, None, None),
    ('c', 'X', 1, 2, None, None),
    ('c', 'Y', 1, 2, None, None),
]
ORDER = [(0, 0), (0, 1), (0, 3), (1, 0), (1, 1), (1, 3), (0, 2), (1, 2)]
FIRST = [('send', 33), ('send', 34), ('send', 41), ('send', 1), ('send', 4), ('send', 8), ('send', 9), ('send', 0), ('send', 42), ('send', 37)]
BEFORE_LEFT = [
    [],
    [],
    [],
    [],
]
BEFORE_AMPS = [
    [],
    [],
    [],
    [],
    [],
    [('wait', 33), ('send', 35), ('send', 47), ('wait', 34), ('send', 36), ('send', 45), ('wait', 41), ('wait', 1), ('send', 12), ('send', 3), ('send', 5), ('send', 48), ('send', 39), ('wait', 4), ('send', 22)],
    [],
    [],
    [],
    [],
    [('wait', 8), ('wait', 9), ('send', 11), ('wait', 0), ('send', 15), ('send', 16), ('send', 2), ('send', 6), ('send', 10), ('send', 13), ('send', 44), ('wait', 42), ('wait', 37)],
    [],
    [],
    [('wait', 35), ('wait', 36), ('send', 50), ('send', 51), ('send', 40), ('send', 66), ('send', 54), ('send', 38)],
    [],
    [],
]
BEFORE_CHUNK = [
    [('wait', 47), ('wait', 45), ('send', 46), ('wait', 5), ('wait', 12), ('send', 14), ('send', 24), ('send', 21), ('wait', 22), ('send', 23), ('wait', 3), ('wait', 2), ('send', 18), ('send', 7), ('wait', 11), ('wait', 39), ('send', 59), ('send', 60), ('send', 43), ('send', 53), ('wait', 15), ('wait', 48), ('wait', 44), ('wait', 10), ('send', 65), ('wait', 16), ('send', 17), ('wait', 6), ('send', 28), ('send', 25), ('wait', 51), ('send', 68), ('wait', 50), ('send', 70), ('wait', 65), ('wait', 66)],
    [('wait', 14), ('wait', 13), ('send', 67), ('wait', 40), ('send', 63), ('wait', 54), ('wait', 59), ('wait', 24), ('send', 26), ('wait', 23), ('wait', 38), ('send', 56), ('send', 57), ('send', 72), ('send', 62), ('send', 52), ('send', 49), ('send', 61), ('wait', 46), ('wait', 43), ('wait', 21), ('send', 71), ('wait', 17), ('send', 69), ('wait', 7), ('send', 30), ('send', 31), ('send', 27), ('wait', 67), ('wait', 68)],
    [('wait', 60), ('wait', 53), ('send', 55), ('wait', 18), ('send', 20), ('wait', 28), ('send', 29), ('send', 19), ('wait', 69), ('wait', 70)],
    [('wait', 63), ('send', 64), ('wait', 56), ('wait', 26), ('wait', 25), ('send', 73), ('wait', 57), ('send', 58), ('send', 74), ('wait', 62), ('send', 76), ('wait', 71), ('wait', 72)],
    [('wait', 30), ('wait', 31), ('send', 32), ('wait', 52), ('wait', 49), ('send', 78), ('wait', 27), ('wait', 29), ('send', 75), ('wait', 73), ('wait', 74)],
    [('wait', 61), ('wait', 64), ('wait', 20), ('wait', 19), ('send', 77), ('wait', 75), ('wait', 76)],
    [('wait', 55), ('wait', 58), ('send', 80), ('wait', 32), ('send', 79), ('wait', 77), ('wait', 78)],
    [('wait', 79), ('wait', 80)],
]


class Place:
    def __init__(self):
        self.tile, self.chol = lax.axis_index("tile"), lax.axis_index("chol")
        self.core = lax.rem(self.tile, 2)
        self.x = lax.rem(lax.div(self.tile, 2), 4)
        self.y = lax.rem(lax.div(self.tile, 8), 4)
        self.z = lax.div(self.tile, 32)
        self.xy = self.y * 4 + self.x
        self.slab = self.chol * 2 + self.z

    def device(self, z, y, x, core, chol=None):
        return (((z * 4 + y) * 4 + x) * 2 + core, self.chol if chol is None else chol)

    def neighbour(self, link):
        z, y, x, core = self.z, self.y, self.x, self.core
        if link == "z":
            return self.device(1 - z, y, x, core)
        if link == "c":
            return self.device(z, y, x, 1 - core)
        step = 1 if link[1] == "+" else 3
        if link[0] == "x":
            return self.device(z, y, lax.rem(x + step, 4), core)
        return self.device(z, lax.rem(y + step, 4), x, core)

    def in_plane(self, other):
        return self.device(self.z, lax.div(other, 4), lax.rem(other, 4), self.core)

    def on_column(self, other):
        return self.device(lax.rem(other, 2), self.y, self.x, self.core, lax.div(other, 2))


def region(held, at, part, dz, dy, dx, half, core):
    z, y = lax.rem(at.z + dz, 2), lax.rem(at.y + dy, 4)
    x = slice(None) if dx is None else lax.rem(at.x + dx, 4)
    cols = PART[part]
    rows = slice(None) if half is None else pl.ds(2 * half, 2)
    return held.at[rows, z, y, x, core, :, pl.ds(cols[0], cols[1])]


def received(link, dz, dy, dx):
    if link == "z":
        return 1 - dz, dy, dx
    if link == "c":
        return dz, dy, dx
    step = 3 if link[1] == "+" else 1
    if link[0] == "x":
        return dz, dy, (dx + step) % 4
    return dz, (dy + step) % 4, dx


def transfer(at, held, send_sems, recv_sems, number, incoming):
    link, part, dz, dy, dx, half = MOVES[number]
    core = at.core
    if incoming:
        dz, dy, dx = received(link, dz, dy, dx)
        core = 1 - core if link == "c" else core
    block = region(held, at, part, dz, dy, dx, half, core)
    return pltpu.make_async_remote_copy(
        src_ref=block,
        dst_ref=block,
        send_sem=send_sems.at[number],
        recv_sem=recv_sems.at[number],
        device_id=at.neighbour(link),
        device_id_type=MESH,
    )


def chunk_of(at, step):
    dz, dy = 0, 0
    for turn, (above, beside) in enumerate(ORDER):
        dz = jnp.where(step == turn, above, dz)
        dy = jnp.where(step == turn, beside, dy)
    return lax.rem(at.z + dz, 2), lax.rem(at.y + dy, 4)


def kernel(
    chol_a, chol_b, amps, virt, pair, out,
    held, left, amps_in, amps_c, mask, integral, acc,
    halves, plane_out, plane_in, column_out, column_in, left_in,
    heard_sems, send_sems, recv_sems, load_sems, half_sems, plane_sems, column_sems,
):
    at = Place()
    loads = [
        pltpu.make_async_copy(chol_b, held.at[:, at.z, at.y, at.x, at.core], load_sems.at[0]),
        pltpu.make_async_copy(chol_a, left_in, load_sems.at[1]),
    ]
    for piece in range(8):
        rows = pl.ds((piece // 2 + 4 * (piece % 2)) * 32, 32)
        loads.append(pltpu.make_async_copy(amps.at[rows], amps_in.at[rows], load_sems.at[2 + piece]))
    for load in loads:
        load.start()
    barrier = pltpu.get_barrier_semaphore()
    up, down = (at.on_column(lax.rem(at.slab + step, 8)) for step in (1, 7))
    peers = [at.neighbour(link) for link in ("c", "x+", "x-", "y+", "y-")] + [up, down]
    for peer in peers:
        pl.semaphore_signal(barrier, inc=1, device_id=peer, device_id_type=MESH)

    def hear(count):
        if count:
            pl.semaphore_wait(heard_sems.at[count - 1, 0], 1)
            pl.semaphore_wait(heard_sems.at[count - 1, 1], 1)
        if count < 3:
            pl.semaphore_signal(heard_sems.at[count, 0], inc=1, device_id=up, device_id_type=MESH)
            pl.semaphore_signal(heard_sems.at[count, 1], inc=1, device_id=down, device_id_type=MESH)

    def move(kind, number):
        copy = transfer(at, held, send_sems, recv_sems, number, kind == "wait")
        if kind == "send":
            copy.start()
        else:
            copy.wait_recv()

    def moves(table, step):
        for turn, entries in enumerate(table):
            if entries:
                if isinstance(step, int):
                    for kind, number in entries:
                        move(kind, number)
                    continue

                @pl.when(step == turn)
                def _():
                    for kind, number in entries:
                        move(kind, number)

    loads[0].wait()
    pl.semaphore_wait(barrier, len(peers))
    for kind, number in FIRST:
        move(kind, number)
    hear(0)

    def iota(shape, dim):
        return lax.broadcasted_iota(jnp.int32, shape, dim)

    virt_row = jnp.broadcast_to(virt[...], (8, 64)).astype(F32).astype(BF16)
    spread = (lax.div(iota((64, 1024), 1), 16) == iota((64, 1024), 0)).astype(F32).astype(BF16)
    own = (iota((64, 1024), 0) == at.tile).astype(F32).astype(BF16)
    label = jnp.dot(virt_row, spread, preferred_element_type=F32).astype(jnp.int32)
    mine = jnp.dot(virt_row, own, preferred_element_type=F32).astype(jnp.int32)
    wanted = jnp.bitwise_xor(label, mine)[:1]
    row = iota((256, 256), 0)
    source = (
        lax.rem(lax.div(row, 4), 2) * 128 + lax.div(row, 16) * 8
        + lax.rem(lax.div(row, 8), 2) * 4 + lax.rem(row, 4)
    )
    order = (iota((256, 256), 1) == source).astype(F32).astype(BF16)
    pair_row = jnp.broadcast_to(pair[...], (128, 256)).astype(F32).astype(BF16)
    pair_col = lax.dot_general(order, pair_row, NT, preferred_element_type=F32).astype(jnp.int32)
    for chunk in range(CHUNKS):
        cols = slice(chunk * 128, (chunk + 1) * 128)
        mask[chunk] = (pair_col == wanted[:, cols]).astype(F32).astype(BF16)
    acc[...] = jnp.zeros_like(acc)

    loads[1].wait()

    @pl.loop(0, 4)
    def _(group):
        moves(BEFORE_LEFT, group)
        rows = pl.ds(pl.multiple_of(group * 16, 16), 16)
        for cols in range(0, 1024, 128):
            block = left_in[rows, :, cols : cols + 128]
            left[:, rows, cols : cols + 128] = jnp.swapaxes(block, 0, 1)

    @pl.loop(0, 16)
    def _(group):
        for piece in range(4):

            @pl.when(group == 4 * piece)
            def _():
                loads[2 + 2 * piece].wait()
                loads[3 + 2 * piece].wait()

        for turn in (1, 2):

            @pl.when(group == 7 * turn)
            def _():
                hear(turn)

        moves(BEFORE_AMPS, group)
        rows = pl.ds(pl.multiple_of(group * 16, 16), 16)
        for chunk in range(CHUNKS):
            cols = slice(chunk * 128, (chunk + 1) * 128)
            block = jnp.concatenate(
                [
                    amps_in[pl.ds(128 * z + group * 8 + 4 * core, 4), :, cols]
                    for core in range(2)
                    for z in range(2)
                ],
                0,
            )
            amps_c[chunk, :, rows, :] = jnp.swapaxes(block, 0, 1) * mask[chunk, rows, :][None]

    def multiply(step):
        z, y = chunk_of(at, step)
        for half in range(2):
            vectors = held[2 * half : 2 * half + 2, z, y].reshape(256, 1024)
            block = lax.dot_general(
                left[...].reshape(1024, 1024), vectors, NT, preferred_element_type=F32
            ).astype(BF16)
            for c in range(16):
                for b in range(2):
                    integral[lax.rem(step, 2), pl.ds((2 * half + b) * 64, 64), pl.ds(c * 128, 128)] = (
                        block[c * 64 : (c + 1) * 64, b * 128 : (b + 1) * 128]
                    )

    def fold(step):
        z, y = chunk_of(at, step)
        masked = jnp.concatenate([amps_c[z * 4 + y, c] for c in range(16)], 1)
        acc[...] += lax.dot_general(
            masked, integral[lax.rem(step, 2)], NT, preferred_element_type=F32
        ).reshape(16, 2, 8, 256)

    moves(BEFORE_CHUNK[:1], 0)
    multiply(0)
    hear(3)

    @pl.loop(1, CHUNKS)
    def _(step):
        moves([[]] + BEFORE_CHUNK[1:], step)
        fold(step - 1)
        multiply(step)

    fold(CHUNKS - 1)

    swap = pltpu.make_async_remote_copy(
        src_ref=acc.at[:, 1 - at.core],
        dst_ref=halves,
        send_sem=half_sems.at[0],
        recv_sem=half_sems.at[1],
        device_id=at.neighbour("c"),
        device_id_type=MESH,
    )
    swap.start()
    turn = (
        (lax.rem(iota((256, 256), 0), 64) == lax.div(iota((256, 256), 1), 4))
        & (lax.div(iota((256, 256), 0), 64) == lax.rem(iota((256, 256), 1), 4))
    ).astype(F32).astype(BF16)
    swap.wait_recv()
    pairs = (acc[:, at.core] + halves[...]).reshape(128, 256).astype(BF16)
    pairs = jnp.dot(pairs, turn, preferred_element_type=F32).reshape(16, 8, 256)
    plane_out[...] = jnp.concatenate([pairs[:, :, :128], pairs[:, :, 128:]], 1).astype(BF16)
    copies = []
    far_first = [(dy, dx) for dy in (2, 1, 3, 0) for dx in (2, 1, 3, 0) if dy or dx]
    far_first.sort(key=lambda d: min(d[0], 4 - d[0]) + min(d[1], 4 - d[1]), reverse=True)
    others = [lax.rem(at.y + dy, 4) * 4 + lax.rem(at.x + dx, 4) for dy, dx in far_first]
    for other in others:
        copies.append(
            pltpu.make_async_remote_copy(
                src_ref=plane_out.at[other],
                dst_ref=plane_in.at[at.xy],
                send_sem=plane_sems.at[0, other],
                recv_sem=plane_sems.at[1, at.xy],
                device_id=at.in_plane(other),
                device_id_type=MESH,
            )
        )
        copies[-1].start()
    total = plane_out[at.xy].astype(F32)
    for other in others:
        pltpu.make_async_remote_copy(
            src_ref=plane_out.at[other],
            dst_ref=plane_in.at[other],
            send_sem=plane_sems.at[0, other],
            recv_sem=plane_sems.at[1, other],
            device_id=at.in_plane(other),
            device_id_type=MESH,
        ).wait_recv()
        total += plane_in[other].astype(F32)
    column_out[...] = total.astype(BF16)
    others = [lax.rem(at.slab + step, 8) for step in (4, 3, 5, 2, 6, 1, 7)]
    for other in others:
        copies.append(
            pltpu.make_async_remote_copy(
                src_ref=column_out,
                dst_ref=column_in.at[at.slab],
                send_sem=column_sems.at[0, other],
                recv_sem=column_sems.at[1, at.slab],
                device_id=at.on_column(other),
                device_id_type=MESH,
            )
        )
        copies[-1].start()
    total = column_out[...].astype(F32)
    for other in others:
        pltpu.make_async_remote_copy(
            src_ref=column_out,
            dst_ref=column_in.at[other],
            send_sem=column_sems.at[0, other],
            recv_sem=column_sems.at[1, other],
            device_id=at.on_column(other),
            device_id_type=MESH,
        ).wait_recv()
        total += column_in[other].astype(F32)
    total = jnp.where(at.z == 0, total.reshape(2, 2, 4, 128)[:, 0], total.reshape(2, 2, 4, 128)[:, 1])
    out[:, :128] = total[0]
    out[:, 128:] = total[1]
    for number in range(len(MOVES)):
        transfer(at, held, send_sems, recv_sems, number, False).wait_send()
    swap.wait_send()
    for copy in copies:
        copy.wait_send()


def body(chol_a, chol_b, amplitudes, virt_irrep, pair_irrep):
    vec, a_rows, c_rows = chol_a.shape
    b_rows = chol_b.shape[1]
    pairs, _, virt = amplitudes.shape
    anywhere = pl.BlockSpec(memory_space=pl.ANY)
    inside = pl.BlockSpec(memory_space=pltpu.VMEM)
    dma = pltpu.SemaphoreType.DMA
    return pl.pallas_call(
        kernel,
        out_shape=jax.ShapeDtypeStruct((4, 256), F32),
        in_specs=[anywhere, anywhere, anywhere, inside, inside],
        out_specs=inside,
        scratch_shapes=[
            pltpu.VMEM((b_rows, 2, 4, 4, 2, 16, vec), BF16),
            pltpu.VMEM((c_rows, a_rows, vec), BF16),
            pltpu.VMEM((pairs, c_rows, virt), BF16),
            pltpu.VMEM((CHUNKS, c_rows, pairs, 128), BF16),
            pltpu.VMEM((CHUNKS, pairs, 128), BF16),
            pltpu.VMEM((2, 256, 2048), BF16),
            pltpu.VMEM((16, 2, 8, 256), F32),
            pltpu.VMEM((16, 8, 256), F32),
            pltpu.VMEM((16, 16, 128), BF16),
            pltpu.VMEM((16, 16, 128), BF16),
            pltpu.VMEM((16, 128), BF16),
            pltpu.VMEM((8, 16, 128), BF16),
            pltpu.VMEM((a_rows, c_rows, vec), BF16),
            pltpu.SemaphoreType.REGULAR((3, 2)),
            dma((len(MOVES),)),
            dma((len(MOVES),)),
            dma((10,)),
            dma((2,)),
            dma((2, 16)),
            dma((2, 8)),
        ],
        compiler_params=pltpu.CompilerParams(
            collective_id=0, has_side_effects=True, vmem_limit_bytes=56 * 2**20
        ),
        name="ladder",
    )(
        jnp.transpose(chol_a, (1, 2, 0)),
        jnp.transpose(chol_b, (1, 2, 0)),
        amplitudes,
        virt_irrep.reshape(1, -1),
        pair_irrep.reshape(1, -1),
    )


def solution(mesh):
    placed = (P("chol", None, "tile"), P("chol", None, "tile"), P(None, "tile", None), P(), P())
    return jax.shard_map(
        body, mesh=mesh, in_specs=placed, out_specs=P("tile", None), check_vma=False
    )
```

```python
import jax
import jax.numpy as jnp
from jax import lax
from jax.experimental import pallas as pl
from jax.experimental.pallas import tpu as pltpu
from jax.sharding import PartitionSpec as P

F32, BF16 = jnp.float32, jnp.bfloat16
MESH = pl.DeviceIdType.MESH
NT = (((1,), (1,)), ((), ()))
CHUNKS = 8
PART = {"X": (0, 512), "Y": (512, 512)}
MOVES = [
    ('y+', 'X', 0, 0, 0, None),
    ('y-', 'X', 0, 0, 0, None),
    ('y+', 'X', 0, 3, 0, 0),
    ('y-', 'X', 0, 1, 0, 1),
    ('z', 'X', 0, 0, 0, None),
    ('z', 'X', 0, 1, 0, None),
    ('z', 'X', 0, 3, 0, None),
    ('z', 'X', 0, 2, 0, None),
    ('x+', 'X', 0, 0, 0, None),
    ('x-', 'X', 0, 0, 0, None),
    ('x+', 'X', 0, 0, 3, 0),
    ('x-', 'X', 0, 0, 1, 1),
    ('x+', 'X', 0, 1, 0, None),
    ('x-', 'X', 0, 1, 0, None),
    ('x+', 'X', 0, 1, 3, None),
    ('x+', 'X', 0, 3, 0, None),
    ('x-', 'X', 0, 3, 0, None),
    ('x-', 'X', 0, 3, 1, None),
    ('x+', 'X', 0, 2, 0, None),
    ('x-', 'X', 0, 2, 0, None),
    ('x+', 'X', 0, 2, 3, None),
    ('x+', 'X', 1, 0, 0, None),
    ('x-', 'X', 1, 0, 0, None),
    ('x-', 'X', 1, 0, 1, None),
    ('x+', 'X', 1, 1, 0, None),
    ('x-', 'X', 1, 1, 0, None),
    ('x+', 'X', 1, 1, 3, None),
    ('x+', 'X', 1, 3, 0, None),
    ('x-', 'X', 1, 3, 0, None),
    ('x-', 'X', 1, 3, 1, None),
    ('x+', 'X', 1, 2, 0, None),
    ('x-', 'X', 1, 2, 0, None),
    ('x-', 'X', 1, 2, 1, None),
    ('x+', 'Y', 0, 0, 0, None),
    ('x-', 'Y', 0, 0, 0, None),
    ('x+', 'Y', 0, 0, 3, 0),
    ('x-', 'Y', 0, 0, 1, 1),
    ('z', 'Y', 0, 0, 0, None),
    ('z', 'Y', 0, 0, 1, None),
    ('z', 'Y', 0, 0, 3, None),
    ('z', 'Y', 0, 0, 2, None),
    ('y+', 'Y', 0, 0, 0, None),
    ('y-', 'Y', 0, 0, 0, None),
    ('y+', 'Y', 0, 3, 0, None),
    ('y+', 'Y', 0, 0, 1, None),
    ('y-', 'Y', 0, 0, 1, None),
    ('y-', 'Y', 0, 1, 1, None),
    ('y+', 'Y', 0, 0, 3, None),
    ('y-', 'Y', 0, 0, 3, None),
    ('y+', 'Y', 0, 3, 3, None),
    ('y+', 'Y', 0, 0, 2, None),
    ('y-', 'Y', 0, 0, 2, None),
    ('y-', 'Y', 0, 1, 2, None),
    ('y+', 'Y', 1, 0, 0, None),
    ('y-', 'Y', 1, 0, 0, None),
    ('y+', 'Y', 1, 3, 0, None),
    ('y+', 'Y', 1, 0, 1, None),
    ('y-', 'Y', 1, 0, 1, None),
    ('y-', 'Y', 1, 1, 1, None),
    ('y+', 'Y', 1, 0, 3, None),
    ('y-', 'Y', 1, 0, 3, None),
    ('y+', 'Y', 1, 3, 3, None),
    ('y+', 'Y', 1, 0, 2, None),
    ('y-', 'Y', 1, 0, 2, None),
    ('y-', 'Y', 1, 1, 2, None),
    ('c', 'X', 0, 0, None, None),
    ('c', 'Y', 0, 0, None, None),
    ('c', 'X', 0, 1, None, None),
    ('c', 'Y', 0, 1, None, None),
    ('c', 'X', 0, 3, None, None),
    ('c', 'Y', 0, 3, None, None),
    ('c', 'X', 1, 0, None, None),
    ('c', 'Y', 1, 0, None, None),
    ('c', 'X', 1, 1, None, None),
    ('c', 'Y', 1, 1, None, None),
    ('c', 'X', 1, 3, None, None),
    ('c', 'Y', 1, 3, None, None),
    ('c', 'X', 0, 2, None, None),
    ('c', 'Y', 0, 2, None, None),
    ('c', 'X', 1, 2, None, None),
    ('c', 'Y', 1, 2, None, None),
]
ORDER = [(0, 0), (0, 1), (0, 3), (1, 0), (1, 1), (1, 3), (0, 2), (1, 2)]
FIRST = [('send', 33), ('send', 34), ('send', 41), ('send', 1), ('send', 4), ('send', 8), ('send', 9), ('send', 0), ('send', 42), ('send', 37)]
BEFORE_LEFT = [
    [],
    [],
    [],
    [],
]
BEFORE_AMPS = [
    [],
    [],
    [],
    [],
    [],
    [('wait', 33), ('send', 35), ('send', 47), ('wait', 34), ('send', 36), ('send', 45), ('wait', 41), ('wait', 1), ('send', 12), ('send', 3), ('send', 5), ('send', 48), ('send', 39), ('wait', 4), ('send', 22)],
    [],
    [],
    [],
    [],
    [('wait', 8), ('wait', 9), ('send', 11), ('wait', 0), ('send', 15), ('send', 16), ('send', 2), ('send', 6), ('send', 10), ('send', 13), ('send', 44), ('wait', 42), ('wait', 37)],
    [],
    [],
    [('wait', 35), ('wait', 36), ('send', 50), ('send', 51), ('send', 40), ('send', 66), ('send', 54), ('send', 38)],
    [],
    [],
]
BEFORE_CHUNK = [
    [('wait', 47), ('wait', 45), ('send', 46), ('wait', 5), ('wait', 12), ('send', 14), ('send', 24), ('send', 21), ('wait', 22), ('send', 23), ('wait', 3), ('wait', 2), ('send', 18), ('send', 7), ('wait', 11), ('wait', 39), ('send', 59), ('send', 60), ('send', 43), ('send', 53), ('wait', 15), ('wait', 48), ('wait', 44), ('wait', 10), ('send', 65), ('wait', 16), ('send', 17), ('wait', 6), ('send', 28), ('send', 25), ('wait', 51), ('send', 68), ('wait', 50), ('send', 70), ('wait', 65), ('wait', 66)],
    [('wait', 14), ('wait', 13), ('send', 67), ('wait', 40), ('send', 63), ('wait', 54), ('wait', 59), ('wait', 24), ('send', 26), ('wait', 23), ('wait', 38), ('send', 56), ('send', 57), ('send', 72), ('send', 62), ('send', 52), ('send', 49), ('send', 61), ('wait', 46), ('wait', 43), ('wait', 21), ('send', 71), ('wait', 17), ('send', 69), ('wait', 7), ('send', 30), ('send', 31), ('send', 27), ('wait', 67), ('wait', 68)],
    [('wait', 60), ('wait', 53), ('send', 55), ('wait', 18), ('send', 20), ('wait', 28), ('send', 29), ('send', 19), ('wait', 69), ('wait', 70)],
    [('wait', 63), ('send', 64), ('wait', 56), ('wait', 26), ('wait', 25), ('send', 73), ('wait', 57), ('send', 58), ('send', 74), ('wait', 62), ('send', 76), ('wait', 71), ('wait', 72)],
    [('wait', 30), ('wait', 31), ('send', 32), ('wait', 52), ('wait', 49), ('send', 78), ('wait', 27), ('wait', 29), ('send', 75), ('wait', 73), ('wait', 74)],
    [('wait', 61), ('wait', 64), ('wait', 20), ('wait', 19), ('send', 77), ('wait', 75), ('wait', 76)],
    [('wait', 55), ('wait', 58), ('send', 80), ('wait', 32), ('send', 79), ('wait', 77), ('wait', 78)],
    [('wait', 79), ('wait', 80)],
]


class Place:
    def __init__(self):
        self.tile, self.chol = lax.axis_index("tile"), lax.axis_index("chol")
        self.core = lax.rem(self.tile, 2)
        self.x = lax.rem(lax.div(self.tile, 2), 4)
        self.y = lax.rem(lax.div(self.tile, 8), 4)
        self.z = lax.div(self.tile, 32)
        self.xy = self.y * 4 + self.x
        self.slab = self.chol * 2 + self.z

    def device(self, z, y, x, core, chol=None):
        return (((z * 4 + y) * 4 + x) * 2 + core, self.chol if chol is None else chol)

    def neighbour(self, link):
        z, y, x, core = self.z, self.y, self.x, self.core
        if link == "z":
            return self.device(1 - z, y, x, core)
        if link == "c":
            return self.device(z, y, x, 1 - core)
        step = 1 if link[1] == "+" else 3
        if link[0] == "x":
            return self.device(z, y, lax.rem(x + step, 4), core)
        return self.device(z, lax.rem(y + step, 4), x, core)

    def in_plane(self, other):
        return self.device(self.z, lax.div(other, 4), lax.rem(other, 4), self.core)

    def on_column(self, other):
        return self.device(lax.rem(other, 2), self.y, self.x, self.core, lax.div(other, 2))


def region(held, at, part, dz, dy, dx, half, core):
    z, y = lax.rem(at.z + dz, 2), lax.rem(at.y + dy, 4)
    x = slice(None) if dx is None else lax.rem(at.x + dx, 4)
    cols = PART[part]
    rows = slice(None) if half is None else pl.ds(2 * half, 2)
    return held.at[rows, z, y, x, core, :, pl.ds(cols[0], cols[1])]


def received(link, dz, dy, dx):
    if link == "z":
        return 1 - dz, dy, dx
    if link == "c":
        return dz, dy, dx
    step = 3 if link[1] == "+" else 1
    if link[0] == "x":
        return dz, dy, (dx + step) % 4
    return dz, (dy + step) % 4, dx


def transfer(at, held, send_sems, recv_sems, number, incoming):
    link, part, dz, dy, dx, half = MOVES[number]
    core = at.core
    if incoming:
        dz, dy, dx = received(link, dz, dy, dx)
        core = 1 - core if link == "c" else core
    block = region(held, at, part, dz, dy, dx, half, core)
    return pltpu.make_async_remote_copy(
        src_ref=block,
        dst_ref=block,
        send_sem=send_sems.at[number],
        recv_sem=recv_sems.at[number],
        device_id=at.neighbour(link),
        device_id_type=MESH,
    )


def chunk_of(at, step):
    dz, dy = 0, 0
    for turn, (above, beside) in enumerate(ORDER):
        dz = jnp.where(step == turn, above, dz)
        dy = jnp.where(step == turn, beside, dy)
    return lax.rem(at.z + dz, 2), lax.rem(at.y + dy, 4)


def kernel(
    chol_a, chol_b, amps, virt, pair, out,
    held, left, amps_in, amps_c, mask, integral, acc,
    halves, plane_out, plane_in, column_out, column_in, left_in,
    heard_sems, send_sems, recv_sems, load_sems, half_sems, plane_sems, column_sems,
):
    at = Place()
    loads = [
        pltpu.make_async_copy(chol_b, held.at[:, at.z, at.y, at.x, at.core], load_sems.at[0]),
        pltpu.make_async_copy(chol_a, left_in, load_sems.at[1]),
    ]
    for piece in range(8):
        rows = pl.ds((piece // 2 + 4 * (piece % 2)) * 32, 32)
        loads.append(pltpu.make_async_copy(amps.at[rows], amps_in.at[rows], load_sems.at[2 + piece]))
    for load in loads:
        load.start()
    barrier = pltpu.get_barrier_semaphore()
    up, down = (at.on_column(lax.rem(at.slab + step, 8)) for step in (1, 7))
    peers = [at.neighbour(link) for link in ("c", "x+", "x-", "y+", "y-")] + [up, down]
    for peer in peers:
        pl.semaphore_signal(barrier, inc=1, device_id=peer, device_id_type=MESH)

    def hear(count):
        if count:
            pl.semaphore_wait(heard_sems.at[count - 1, 0], 1)
            pl.semaphore_wait(heard_sems.at[count - 1, 1], 1)
        if count < 3:
            pl.semaphore_signal(heard_sems.at[count, 0], inc=1, device_id=up, device_id_type=MESH)
            pl.semaphore_signal(heard_sems.at[count, 1], inc=1, device_id=down, device_id_type=MESH)

    def move(kind, number):
        copy = transfer(at, held, send_sems, recv_sems, number, kind == "wait")
        if kind == "send":
            copy.start()
        else:
            copy.wait_recv()

    def moves(table, step):
        for turn, entries in enumerate(table):
            if entries:
                if isinstance(step, int):
                    for kind, number in entries:
                        move(kind, number)
                    continue

                @pl.when(step == turn)
                def _():
                    for kind, number in entries:
                        move(kind, number)

    loads[0].wait()
    pl.semaphore_wait(barrier, len(peers))
    for kind, number in FIRST:
        move(kind, number)
    hear(0)

    def iota(shape, dim):
        return lax.broadcasted_iota(jnp.int32, shape, dim)

    virt_row = jnp.broadcast_to(virt[...], (8, 64)).astype(F32).astype(BF16)
    spread = (lax.div(iota((64, 1024), 1), 16) == iota((64, 1024), 0)).astype(F32).astype(BF16)
    own = (iota((64, 1024), 0) == at.tile).astype(F32).astype(BF16)
    label = jnp.dot(virt_row, spread, preferred_element_type=F32).astype(jnp.int32)
    mine = jnp.dot(virt_row, own, preferred_element_type=F32).astype(jnp.int32)
    wanted = jnp.bitwise_xor(label, mine)[:1]
    row = iota((256, 256), 0)
    source = (
        lax.rem(lax.div(row, 4), 2) * 128 + lax.div(row, 16) * 8
        + lax.rem(lax.div(row, 8), 2) * 4 + lax.rem(row, 4)
    )
    order = (iota((256, 256), 1) == source).astype(F32).astype(BF16)
    pair_row = jnp.broadcast_to(pair[...], (128, 256)).astype(F32).astype(BF16)
    pair_col = lax.dot_general(order, pair_row, NT, preferred_element_type=F32).astype(jnp.int32)
    for chunk in range(CHUNKS):
        cols = slice(chunk * 128, (chunk + 1) * 128)
        mask[chunk] = (pair_col == wanted[:, cols]).astype(F32).astype(BF16)
    acc[...] = jnp.zeros_like(acc)

    loads[1].wait()

    @pl.loop(0, 4)
    def _(group):
        moves(BEFORE_LEFT, group)
        rows = pl.ds(pl.multiple_of(group * 16, 16), 16)
        for cols in range(0, 1024, 128):
            block = left_in[rows, :, cols : cols + 128]
            left[:, rows, cols : cols + 128] = jnp.swapaxes(block, 0, 1)

    @pl.loop(0, 16)
    def _(group):
        for piece in range(4):

            @pl.when(group == 4 * piece)
            def _():
                loads[2 + 2 * piece].wait()
                loads[3 + 2 * piece].wait()

        for turn in (1, 2):

            @pl.when(group == 7 * turn)
            def _():
                hear(turn)

        moves(BEFORE_AMPS, group)
        rows = pl.ds(pl.multiple_of(group * 16, 16), 16)
        for chunk in range(CHUNKS):
            cols = slice(chunk * 128, (chunk + 1) * 128)
            block = jnp.concatenate(
                [
                    amps_in[pl.ds(128 * z + group * 8 + 4 * core, 4), :, cols]
                    for core in range(2)
                    for z in range(2)
                ],
                0,
            )
            amps_c[chunk, :, rows, :] = jnp.swapaxes(block, 0, 1) * mask[chunk, rows, :][None]

    def multiply(step):
        z, y = chunk_of(at, step)
        for half in range(2):
            vectors = held[2 * half : 2 * half + 2, z, y].reshape(256, 1024)
            block = lax.dot_general(
                left[...].reshape(1024, 1024), vectors, NT, preferred_element_type=F32
            ).astype(BF16)
            for c in range(16):
                for b in range(2):
                    integral[lax.rem(step, 2), pl.ds((2 * half + b) * 64, 64), pl.ds(c * 128, 128)] = (
                        block[c * 64 : (c + 1) * 64, b * 128 : (b + 1) * 128]
                    )

    def fold(step):
        z, y = chunk_of(at, step)
        masked = jnp.concatenate([amps_c[z * 4 + y, c] for c in range(16)], 1)
        acc[...] += lax.dot_general(
            masked, integral[lax.rem(step, 2)], NT, preferred_element_type=F32
        ).reshape(16, 2, 8, 256)

    moves(BEFORE_CHUNK[:1], 0)
    multiply(0)
    hear(3)

    @pl.loop(1, CHUNKS)
    def _(step):
        moves([[]] + BEFORE_CHUNK[1:], step)
        fold(step - 1)
        multiply(step)

    fold(CHUNKS - 1)

    swap = pltpu.make_async_remote_copy(
        src_ref=acc.at[:, 1 - at.core],
        dst_ref=halves,
        send_sem=half_sems.at[0],
        recv_sem=half_sems.at[1],
        device_id=at.neighbour("c"),
        device_id_type=MESH,
    )
    swap.start()
    swap.wait_recv()
    pairs = acc[:, at.core] + halves[...]
    plane_out[...] = jnp.concatenate([pairs[:, :, :128], pairs[:, :, 128:]], 1).astype(BF16)
    copies = []
    far_first = [(dy, dx) for dy in (2, 1, 3, 0) for dx in (2, 1, 3, 0) if dy or dx]
    far_first.sort(key=lambda d: min(d[0], 4 - d[0]) + min(d[1], 4 - d[1]), reverse=True)
    others = [lax.rem(at.y + dy, 4) * 4 + lax.rem(at.x + dx, 4) for dy, dx in far_first]
    for other in others:
        copies.append(
            pltpu.make_async_remote_copy(
                src_ref=plane_out.at[other],
                dst_ref=plane_in.at[at.xy],
                send_sem=plane_sems.at[0, other],
                recv_sem=plane_sems.at[1, at.xy],
                device_id=at.in_plane(other),
                device_id_type=MESH,
            )
        )
        copies[-1].start()
    total = plane_out[at.xy].astype(F32)
    for other in others:
        pltpu.make_async_remote_copy(
            src_ref=plane_out.at[other],
            dst_ref=plane_in.at[other],
            send_sem=plane_sems.at[0, other],
            recv_sem=plane_sems.at[1, other],
            device_id=at.in_plane(other),
            device_id_type=MESH,
        ).wait_recv()
        total += plane_in[other].astype(F32)
    column_out[...] = total.astype(BF16)
    others = [lax.rem(at.slab + step, 8) for step in (4, 3, 5, 2, 6, 1, 7)]
    for other in others:
        copies.append(
            pltpu.make_async_remote_copy(
                src_ref=column_out,
                dst_ref=column_in.at[at.slab],
                send_sem=column_sems.at[0, other],
                recv_sem=column_sems.at[1, at.slab],
                device_id=at.on_column(other),
                device_id_type=MESH,
            )
        )
        copies[-1].start()
    total = column_out[...].astype(F32)
    for other in others:
        pltpu.make_async_remote_copy(
            src_ref=column_out,
            dst_ref=column_in.at[other],
            send_sem=column_sems.at[0, other],
            recv_sem=column_sems.at[1, other],
            device_id=at.on_column(other),
            device_id_type=MESH,
        ).wait_recv()
        total += column_in[other].astype(F32)
    total = jnp.where(at.z == 0, total.reshape(2, 2, 4, 128)[:, 0], total.reshape(2, 2, 4, 128)[:, 1])
    out[:, :128] = total[0]
    out[:, 128:] = total[1]
    for number in range(len(MOVES)):
        transfer(at, held, send_sems, recv_sems, number, False).wait_send()
    swap.wait_send()
    for copy in copies:
        copy.wait_send()


def body(chol_a, chol_b, amplitudes, virt_irrep, pair_irrep):
    vec, a_rows, c_rows = chol_a.shape
    b_rows = chol_b.shape[1]
    pairs, _, virt = amplitudes.shape
    anywhere = pl.BlockSpec(memory_space=pl.ANY)
    inside = pl.BlockSpec(memory_space=pltpu.VMEM)
    dma = pltpu.SemaphoreType.DMA
    sums = pl.pallas_call(
        kernel,
        out_shape=jax.ShapeDtypeStruct((4, 256), F32),
        in_specs=[anywhere, anywhere, anywhere, inside, inside],
        out_specs=inside,
        scratch_shapes=[
            pltpu.VMEM((b_rows, 2, 4, 4, 2, 16, vec), BF16),
            pltpu.VMEM((c_rows, a_rows, vec), BF16),
            pltpu.VMEM((pairs, c_rows, virt), BF16),
            pltpu.VMEM((CHUNKS, c_rows, pairs, 128), BF16),
            pltpu.VMEM((CHUNKS, pairs, 128), BF16),
            pltpu.VMEM((2, 256, 2048), BF16),
            pltpu.VMEM((16, 2, 8, 256), F32),
            pltpu.VMEM((16, 8, 256), F32),
            pltpu.VMEM((16, 16, 128), BF16),
            pltpu.VMEM((16, 16, 128), BF16),
            pltpu.VMEM((16, 128), BF16),
            pltpu.VMEM((8, 16, 128), BF16),
            pltpu.VMEM((a_rows, c_rows, vec), BF16),
            pltpu.SemaphoreType.REGULAR((3, 2)),
            dma((len(MOVES),)),
            dma((len(MOVES),)),
            dma((10,)),
            dma((2,)),
            dma((2, 16)),
            dma((2, 8)),
        ],
        compiler_params=pltpu.CompilerParams(
            collective_id=0, has_side_effects=True, vmem_limit_bytes=56 * 2**20
        ),
        name="ladder",
    )(
        jnp.transpose(chol_a, (1, 2, 0)),
        jnp.transpose(chol_b, (1, 2, 0)),
        amplitudes,
        virt_irrep.reshape(1, -1),
        pair_irrep.reshape(1, -1),
    )
    return sums.reshape(4, b_rows, a_rows).transpose(0, 2, 1).reshape(4, a_rows * b_rows)


def solution(mesh):
    placed = (P("chol", None, "tile"), P("chol", None, "tile"), P(None, "tile", None), P(), P())
    return jax.shard_map(
        body, mesh=mesh, in_specs=placed, out_specs=P("tile", None), check_vma=False
    )
```
